1024 devices in a mesh: fsdp: 256 (over z, y, core), tp: 4 (over x).
Axes of the slice: x: 4, y: 4, z: 32, core: 2. Of those that a mesh axis runs over, the one named last changes fastest.
Arguments:
- momentum: float32 [28672, 8192], P('fsdp', 'tp'), may hold values from -200 to 200
- gradient: bfloat16 [28672, 8192], P('fsdp', 'tp'), may hold values from -24 to 24
- basis: float32 [8192, 256], P('tp'), may hold values from -0.0625 to 0.0625
Outputs:
- new_momentum: float32 [28672, 8192], P('fsdp', 'tp')
- q_next: float32 [8192, 256], P(('tp', 'fsdp'))
- direction: float32 [28672, 8192], P('fsdp', 'tp')
The draws below stay inside these ranges and needn't reach their ends.
All inputs are finite; a program needn't handle non-finite values.
Results may differ from the reference program's by a relative error of at most 0.0003.
Values sent between devices are 32-bit elements; how exact they have to be, the bound alone decides.
No kernel may reach another device: no remote copies, remote signals or barrier semaphores. Data moves between devices by JAX's collectives and lax.ppermute only.
A program may use at most 32 MiB of HBM per device.

```python
import math
import jax
import jax.numpy as jnp
from jax import lax

D = 8192
FF = 28672
RANK = 256


def draw_momentum(key, part):
    key = jax.random.fold_in(key, 7)
    key_base, key_rows, key_cols = jax.random.split(key, 3)
    base = jnp.clip(jax.random.normal(key_base, (FF, D), jnp.float32), -4.0, 4.0)
    rise_log = math.log(3.0)
    position = jnp.arange(FF, dtype=jnp.float32)[:, None] / FF
    row_scale = jnp.exp(math.log(10.0) * jax.random.uniform(key_rows, (FF, 1), jnp.float32) + rise_log * position)
    col_scale = jnp.exp(math.log(10.0) * jax.random.uniform(key_cols, (1, D), jnp.float32))
    return base * row_scale * col_scale / 20.0


def raised(result, own_key, source, target, parts, factor):
    def block_of(dim):
        return (jnp.arange(result.shape[dim]) // (result.shape[dim] // parts)).reshape((-1,) + (1,) * (result.ndim - 1 - dim))

    first = jax.random.permutation(own_key, parts)[block_of(target)]
    second = (block_of(target) + parts // 2) % parts
    return jnp.where((block_of(source) == first) | (block_of(source) == second), factor * result, result)


def block_levels(key, shape, shards, least, largest):
    gain, own = 1.0, jax.random.fold_in(key, 6)
    for dim, shards_of in shards:
        draws = jnp.exp(jax.random.uniform(jax.random.fold_in(own, dim), (shards_of,), jnp.float32, least / len(shards), largest / len(shards)))
        gain = gain * jnp.repeat(draws, shape[dim] // shards_of).reshape([-1 if axis == dim else 1 for axis in range(len(shape))])
    return gain


def bell_draw(rng, shape, spread, most, pieces=(), kind=jnp.bfloat16):
    entries = spread * jax.random.normal(rng, shape, jnp.float32)
    if pieces:
        entries = entries * block_levels(rng, shape, pieces, -0.22, 0.18)
    return jnp.clip(entries, -most, most).astype(kind)


def gaussian_with(key, extent, scale, most, cuts, heavy, kind=jnp.bfloat16):
    drawn = scale * jax.random.normal(key, extent, jnp.float32)
    if cuts:
        drawn = drawn * block_levels(key, extent, cuts, -0.22, 0.18)
    return jnp.clip(raised(drawn, jax.random.fold_in(key, 3), *heavy), -most, most).astype(kind)


def setup_inputs(seed: int = 0) -> dict:
    key_of = jax.random.split(jax.random.key(seed), 4)
    momentum = draw_momentum(jax.random.fold_in(key_of[3], 71), 0)
    gradient = gaussian_with(key_of[1], (FF, D), 1.0, 24.0, ((0, 256), (1, 4)), (0, 1, 256, 6.0))
    basis = bell_draw(key_of[2], (D, RANK), D ** -0.5, 0.0625, ((0, 4),), jnp.float32)
    return {"momentum": momentum, "gradient": gradient, "basis": basis}


def reference(momentum, gradient, basis):
    highest = lax.Precision.HIGHEST
    buffer = momentum + gradient.astype(jnp.float32)
    left_factor = jnp.dot(buffer.astype(jnp.float32), basis.astype(jnp.float32), precision=highest, preferred_element_type=jnp.float32)
    gram = jnp.dot(left_factor.T.astype(jnp.float32), left_factor.astype(jnp.float32), precision=highest, preferred_element_type=jnp.float32)
    gram = gram + 1.0 * FF * jnp.eye(RANK, dtype=jnp.float32)
    factor = jnp.linalg.cholesky(gram)
    orthonormal = lax.linalg.triangular_solve(factor, left_factor, left_side=False, lower=True, transpose_a=True)
    right_factor = jnp.dot(buffer.T.astype(jnp.float32), orthonormal.astype(jnp.float32), precision=highest, preferred_element_type=jnp.float32)
    col_norms = jnp.sqrt(lax.optimization_barrier(jnp.sum(right_factor * right_factor, axis=0)) + 1e-06)
    q_next = right_factor / col_norms[None, :]
    new_momentum = buffer - 0.05 * jnp.dot(orthonormal.astype(jnp.float32), right_factor.T.astype(jnp.float32), precision=highest, preferred_element_type=jnp.float32)
    dir_scale = math.sqrt(FF * D / RANK)
    direction = dir_scale * jnp.dot(orthonormal.astype(jnp.float32), q_next.T.astype(jnp.float32), precision=highest, preferred_element_type=jnp.float32)
    return (new_momentum, q_next, direction)
```

```python
import math

import jax
import jax.numpy as jnp
from jax import lax
from jax.experimental import pallas as pl
from jax.experimental.pallas import tpu as pltpu
from jax.sharding import Mesh, PartitionSpec as P

D = 8192
FF = 28672
RANK = 256
SIZES = {"zh": 4, "zl": 8, "y": 4, "c": 2, "tp": 4}
ROWS = ("zh", "zl", "y", "c")
HIGHEST = lax.Precision.HIGHEST
F32 = jnp.float32
FIRST = (((0,), (0,)), ((), ()))
LAST = (((1,), (1,)), ((), ()))
STEPS = 2
SIDE = 64
GROUP = 8
PARAMS = pltpu.CompilerParams(vmem_limit_bytes=12 * 2**20)


def dot(a, b, dims):
    return lax.dot_general(a, b, dims, precision=HIGHEST, preferred_element_type=F32)


def exchange(blocks, axis):
    return lax.all_to_all(blocks, axis, 0, 0, tiled=True)


def left_products(momentum_hbm, gradient_hbm, basis_hbm, out_ref, buffer_ref, gradient_ref, basis_ref, sems):
    part = buffer_ref.shape[1] // STEPS
    copies = []
    for i in range(STEPS):
        cols = pl.ds(i * part, part)
        pairs = (
            (basis_hbm.at[cols, :], basis_ref.at[cols, :]),
            (momentum_hbm.at[:, cols], buffer_ref.at[:, cols]),
            (gradient_hbm.at[:, cols], gradient_ref.at[:, cols]),
        )
        copies.append([pltpu.make_async_copy(src, dst, sems.at[i, k]) for k, (src, dst) in enumerate(pairs)])
        for copy in copies[i]:
            copy.start()
    total = None
    for i in range(STEPS):
        for copy in copies[i]:
            copy.wait()
        cols = slice(i * part, (i + 1) * part)
        buffer = buffer_ref[:, cols] + gradient_ref[:, cols].astype(F32)
        buffer_ref[:, cols] = buffer
        product = dot(buffer, basis_ref[cols, :], (((1,), (0,)), ((), ())))
        total = product if total is None else total + product
    for i in range(out_ref.shape[0]):
        out_ref[i] = total


def local_products(core_ref, parts_ref, buffer_ref, left_ref, keep_ref, send_ref):
    first = core_ref[0] == 0
    left = (parts_ref[0] + parts_ref[1]) + (parts_ref[2] + parts_ref[3])
    left_ref[...] = left

    def put(y, zl, tile, blocks):
        keep_ref[y, zl, tile * 8 : tile * 8 + 8, :] = jnp.where(first, blocks[0], blocks[1])
        send_ref[y, zl, tile * 8 : tile * 8 + 8, :] = jnp.where(first, blocks[1], blocks[0])

    gram = dot(left, left, FIRST)
    for y in range(4):
        for zl in range(8):
            at = (y * 8 + zl) // 2 * 8
            lanes = slice(zl % 2 * 128, zl % 2 * 128 + 128)
            blocks = [gram[c * 128 + at : c * 128 + at + 8, lanes] for c in range(2)]
            put(y, zl, 8, blocks)
    for zh in range(4):
        cols = slice(zh * 512, (zh + 1) * 512)
        rows = dot(buffer_ref[:, cols], left, FIRST).reshape(8, 4, 2, 8, RANK)
        for y in range(4):
            for zl in range(8):
                for half in range(2):
                    lanes = slice(half * 128, half * 128 + 128)
                    put(y, zl, zh * 2 + half, [rows[zl, y, 0][:, lanes], rows[zl, y, 1][:, lanes]])


def add(a_ref, b_ref, out_ref):
    out_ref[...] = a_ref[...] + b_ref[...]


def sum_first(parts_ref, out_ref):
    total = parts_ref[0]
    for i in range(1, parts_ref.shape[0]):
        total += parts_ref[i]
    out_ref[...] = total


def sum_and_copy(parts_ref, out_ref):
    total = parts_ref[0]
    for i in range(1, parts_ref.shape[0]):
        total += parts_ref[i]
    for i in range(out_ref.shape[0]):
        out_ref[i] = total


def copies(block_ref, out_ref):
    block = block_ref[...]
    for i in range(out_ref.shape[0]):
        out_ref[i] = block


def inverse_of_block(block, eye):
    tile = jnp.concatenate([block, eye], axis=1)
    full = tile.shape
    row_id = lax.broadcasted_iota(jnp.int32, full, 0)

    def wide(v):
        return jnp.broadcast_to(v, full)

    def flat(v):
        return jnp.broadcast_to(v, (1, full[1]))

    for j in range(0, SIDE, GROUP):
        rows = [tile[j + a : j + a + 1, :] for a in range(GROUP)]
        cols = [wide(tile[:, j + a : j + a + 1]) for a in range(GROUP)]
        p = {(a, b): flat(rows[a][:, j + b : j + b + 1]) for a in range(GROUP) for b in range(a, GROUP)}
        for a in range(GROUP):
            inv = 1.0 / p[a, a]
            for b in range(a + 1, GROUP):
                ratio = p[a, b] * inv
                for d in range(b, GROUP):
                    p[b, d] = p[b, d] - ratio * p[a, d]
                rows[b] = rows[b] - ratio * rows[a]
                cols[b] = cols[b] - cols[a] * wide(ratio)
            tile = tile - jnp.where(row_id > j + a, cols[a], 0.0) * wide(rows[a] * inv)
    pivots = jnp.sum(jnp.where(eye > 0.0, tile[:, :SIDE], 0.0), axis=1, keepdims=True)
    return tile[:, SIDE:] * lax.rsqrt(pivots)


def solve(core_ref, mine_ref, other_ref, left_ref, ortho_ref, right_ref, squares_ref, work):
    halves_of = ((core_ref[0], mine_ref), (1 - core_ref[0], other_ref))
    for c, ref in halves_of:
        for y in range(4):
            for zl in range(8):
                at = pl.ds(pl.multiple_of(c * 128 + (y * 8 + zl) // 2 * 8, 8), 8)
                work[at, zl % 2 * 128 : zl % 2 * 128 + 128] = ref[y, zl, 64:72, :]
    r = lax.broadcasted_iota(jnp.int32, (RANK, RANK), 0)
    c = lax.broadcasted_iota(jnp.int32, (RANK, RANK), 1)
    work[...] += jnp.where(r == c, 1.0 * FF, 0.0)
    r = lax.broadcasted_iota(jnp.int32, (SIDE, SIDE), 0)
    c = lax.broadcasted_iota(jnp.int32, (SIDE, SIDE), 1)
    eye = jnp.where(r == c, 1.0, 0.0)
    lane = lax.broadcasted_iota(jnp.int32, (1, RANK), 1)
    for lo in range(0, RANK, SIDE):
        hi = lo + SIDE
        rows = work[lo:hi, :]
        inverse = inverse_of_block(rows[:, lo:hi], eye)
        inside = (lane >= lo) & (lane < hi)
        pieces = [jnp.zeros((SIDE, lo), F32)] * (lo > 0) + [eye] + [jnp.zeros((SIDE, RANK - hi), F32)] * (hi < RANK)
        rows = jnp.where(inside, jnp.concatenate(pieces, axis=1), rows)
        rows = dot(inverse, rows, (((1,), (0,)), ((), ())))
        work[lo:hi, :] = jnp.where(lane < hi, rows, 0.0)
        if hi < RANK:
            work[hi:, :] = jnp.where(inside, 0.0, work[hi:, :]) - dot(rows[:, hi:], rows, FIRST)
    inverse = work[...]
    ortho_ref[...] = dot(left_ref[...], inverse, LAST)
    squares = jnp.zeros((1, RANK), F32)
    for c, ref in halves_of:
        for y in range(4):
            raw = ref[y, :, 0:64, :].reshape(8, 4, 2, 8, 128)
            raw = jnp.concatenate([raw[:, :, 0], raw[:, :, 1]], axis=-1).reshape(8 * 32, RANK)
            right = dot(raw, inverse, LAST)
            squares += jnp.sum(right * right, axis=0, keepdims=True)
            right = right.reshape(8, 4, 8, RANK)
            for zl in range(8):
                for zh in range(4):
                    at = pl.multiple_of(zh * 512 + (zl * 4 + y) * 16 + c * 8, 8)
                    right_ref[pl.ds(at, 8), :] = right[zl, zh]
    squares_ref[...] = jnp.broadcast_to(squares, squares_ref.shape)


def halves(value):
    high = value.astype(jnp.bfloat16)
    return high, (value - high.astype(F32)).astype(jnp.bfloat16)


def outer(a_high, a_low, b):
    b_high, b_low = b

    def product(x, y):
        return lax.dot_general(x, y, LAST, preferred_element_type=F32)

    return product(a_high, b_high) + (product(a_high, b_low) + product(a_low, b_high))


def finish(place_ref, squares_ref, buffer_ref, ortho_ref, right_ref, momentum_ref, direction_ref, q_ref):
    squares = (squares_ref[0] + squares_ref[1]) + (squares_ref[2] + squares_ref[3])
    norms = jnp.sqrt(squares + 1e-06)
    own = pl.ds(pl.multiple_of(place_ref[0] * 8, 8), 8)
    q_ref[...] = right_ref[own, :] / norms
    ortho = ortho_ref[...]
    high, low = halves(ortho)
    scaled_high, scaled_low = halves(math.sqrt(FF * D / RANK) * ortho / norms[0:1, :])
    for i in range(8):
        cols = slice(i * 256, (i + 1) * 256)
        right = halves(right_ref[cols, :])
        momentum_ref[:, cols] = buffer_ref[:, cols] - 0.05 * outer(high, low, right)
        direction_ref[:, cols] = outer(scaled_high, scaled_low, right)


def shape(*dims):
    return jax.ShapeDtypeStruct(dims, F32)


def call(kernel, out_shape, *args, scalars=0, **options):
    specs = [pl.BlockSpec(memory_space=pltpu.SMEM)] * scalars
    specs += [pl.BlockSpec(memory_space=pltpu.VMEM)] * (len(args) - scalars)
    return pl.pallas_call(
        kernel, out_shape=out_shape, in_specs=specs, compiler_params=PARAMS, name=kernel.__name__, **options
    )(*args)


def shards(momentum, gradient, basis):
    height, width = momentum.shape
    core = lax.axis_index("c").astype(jnp.int32).reshape(1)
    place = lax.axis_index(ROWS).astype(jnp.int32).reshape(1)
    partial_left, buffer = pl.pallas_call(
        left_products,
        in_specs=[pl.BlockSpec(memory_space=pltpu.HBM)] * 3,
        out_specs=[pl.BlockSpec(memory_space=pltpu.VMEM)] * 2,
        out_shape=[shape(4, height, RANK), shape(height, width)],
        scratch_shapes=[
            pltpu.VMEM(gradient.shape, gradient.dtype),
            pltpu.VMEM(basis.shape, F32),
            pltpu.SemaphoreType.DMA((STEPS, 3)),
        ],
        compiler_params=pltpu.CompilerParams(vmem_limit_bytes=58 * 2**20),
        name="left_products",
    )(momentum, gradient, basis)
    parts = exchange(partial_left, "tp")
    block = shape(4, 8, 72, 128)
    left, keep, send = call(
        local_products, [shape(height, RANK), block, block], core, parts, buffer, scalars=1
    )

    swap = ((0, 1), (1, 0))
    sums = call(add, block, keep, lax.ppermute(send, "c", swap))
    sums = call(sum_first, shape(8, 72, 128), exchange(sums, "y"))
    sums = call(sum_and_copy, shape(4, 72, 128), exchange(sums, "zl"))
    sums = call(sum_and_copy, shape(8, 72, 128), exchange(sums, "zh"))
    sums = call(copies, block, exchange(sums, "zl"))
    mine = exchange(sums, "y")
    other = lax.ppermute(mine, "c", swap)

    ortho, right, squares = call(
        solve,
        [shape(height, RANK), shape(width, RANK), shape(4, 8, RANK)],
        core, mine, other, left,
        scalars=1,
        scratch_shapes=[pltpu.VMEM((RANK, RANK), F32)],
    )
    squares = exchange(squares, "tp")
    new_momentum, direction, q_rows = call(
        finish,
        [shape(height, width), shape(height, width), shape(8, RANK)],
        place, squares, buffer, ortho, right,
        scalars=1,
    )
    return (new_momentum, q_rows, direction)


def solution(mesh):
    fine = Mesh(mesh.devices.reshape([SIZES[a] for a in ROWS] + [SIZES["tp"]]), ROWS + ("tp",))
    return jax.shard_map(
        shards,
        mesh=fine,
        in_specs=(P(ROWS, "tp"), P(ROWS, "tp"), P("tp", None)),
        out_specs=(P(ROWS, "tp"), P(("tp",) + ROWS, None), P(ROWS, "tp")),
        check_vma=False,
    )
```
